256 devices in a mesh: pool: 32 (over y, z), blk: 8 (over x, core).
Axes of the slice: x: 4, y: 4, z: 8, core: 2. Of those that a mesh axis runs over, the one named last changes fastest.
Arguments:
- queries: bfloat16 [32768, 4096], P(('pool', 'blk')), may hold values from -7.5 to 7.5
- span_kv: bfloat16 [32768, 1024], P(('pool', 'blk')), may hold values from -6 to 6
- kv_store: bfloat16 [512, 64, 1024], P('pool'), may hold values from -6 to 6
- page_ids: int32 [32, 32], P('pool'), may hold values from 0 to 15
- page_owner: int32 [32, 32], P('pool'), may hold values from 0 to 31, as said below
- prefix_len: int32 [32], P('pool'), may hold values from 1280 to 2048, as said below
Outputs:
- attended: bfloat16 [32768, 4096], P(('pool', 'blk'))
The draws below stay inside these ranges and needn't reach their ends.
Inputs may be any that keep to these rules, and one draw needn't show every extreme that they name: `page_owner`: each request's list names 16 owners, each exactly 2 times; one owner is named by every request. `prefix_len`: some request has a prefix of exactly 2048 tokens.
All inputs are finite; a program needn't handle non-finite values.
Results may differ from the reference program's by a relative error of at most 0.005.
Values may be sent and summed in bfloat16 or wider, within the bound.
A program may use at most 128 MiB of HBM per device.

```python
import math
import jax
import jax.numpy as jnp
from jax import lax

QH = 32
KVH = 4
DH = 128
PAGE = 64
CAP = 2
QB = 128
PAGES_DEV = 16
GROUP = 8
F = 1024
PAGES_REQ = 32
PREFIX = 2048
SPAN = 1024
TOKENS = 32768
N_POOL = 32
N_BLK = 8


def draw_span_kv(key, part):
    key = jax.random.fold_in(key, 11)
    first = jax.random.fold_in(key, 0)
    pairs = jnp.clip(jax.random.normal(first, (TOKENS, 2, KVH, DH), jnp.float32), -6.0, 6.0)
    return pairs.reshape(TOKENS, 2 * KVH * DH).astype(jnp.bfloat16)


def draw_queries(key, part):
    key = jax.random.fold_in(key, 12)
    base = jnp.clip(2.5 * jax.random.normal(key, (TOKENS, KVH, GROUP, DH), jnp.float32), -7.5, 7.5)
    return base.reshape(TOKENS, QH * DH).astype(jnp.bfloat16)


def draw_page_owner(key, part):
    key = jax.random.fold_in(key, 13)
    hot_key, rest = jax.random.split(key)
    hottest = jax.random.randint(hot_key, (), 0, N_POOL)
    request_keys = jax.random.split(rest, N_POOL)
    half = N_POOL // 2

    def one_list(inner):
        pick_key, order_key = jax.random.split(inner)
        others = 1 + jax.random.permutation(pick_key, N_POOL - 1)[:half - 1]
        chosen = (hottest + jnp.concatenate([jnp.zeros((1,), jnp.int32), others.astype(jnp.int32)])) % N_POOL
        listed = jnp.tile(chosen, CAP)
        return listed[jax.random.permutation(order_key, PAGES_REQ)]
    return jax.vmap(one_list)(request_keys).astype(jnp.int32)


def draw_prefix_len(key, part):
    key = jax.random.fold_in(key, 14)
    first, second = jax.random.split(key)
    lengths = jax.random.randint(first, (N_POOL,), 5 * PREFIX // 8, PREFIX + 1)
    longest = jax.random.randint(second, (), 0, N_POOL)
    return jnp.where(jnp.arange(N_POOL) == longest, PREFIX, lengths).astype(jnp.int32)


def set_ends(entries, stream_key, low, largest):
    shape = entries.shape
    index_at = [jax.random.randint(jax.random.fold_in(stream_key, axis), (), 0, shape[axis]) for axis in range(len(shape))]
    entries = entries.at[tuple(index_at)].set(low)
    longest = shape.index(max(shape))
    index_at[longest] = (index_at[longest] + 1) % shape[longest]
    return entries.at[tuple(index_at)].set(largest)


def block_levels(key, extent, shards, low, top_value):
    level, own = 1.0, jax.random.fold_in(key, 6)
    for position, shards_of in shards:
        heights = jnp.exp(jax.random.uniform(jax.random.fold_in(own, position), (shards_of,), jnp.float32, low / len(shards), top_value / len(shards)))
        level = level * jnp.repeat(heights, extent[position] // shards_of).reshape([-1 if axis == position else 1 for axis in range(len(extent))])
    return level


def centred(stream_key, extent, deviation, most, cuts=(), kind=jnp.bfloat16):
    level = block_levels(stream_key, extent, cuts, -0.22, 0.18) if cuts else 1.0
    values = jax.random.normal(stream_key, extent, jnp.float32) * deviation * level
    return jnp.minimum(jnp.maximum(values, -most), most).astype(kind)


def setup_inputs(seed: int = 0) -> dict:
    seeds = jax.random.split(jax.random.key(seed), 7)
    return {
        "queries": draw_queries(jax.random.fold_in(seeds[6], 71), 0),
        "span_kv": draw_span_kv(jax.random.fold_in(seeds[6], 71), 0),
        "kv_store": centred(seeds[2], (N_POOL * PAGES_DEV, PAGE, F), 1.0, 6.0, ((0, 32),)),
        "page_ids": set_ends(jax.random.randint(seeds[3], (N_POOL, PAGES_REQ), 0, PAGES_DEV), jax.random.fold_in(seeds[3], 1), 0, PAGES_DEV - 1).astype(jnp.int32),
        "page_owner": draw_page_owner(jax.random.fold_in(seeds[6], 71), 0),
        "prefix_len": draw_prefix_len(jax.random.fold_in(seeds[6], 71), 0),
    }


def reference(queries, span_kv, kv_store, page_ids, page_owner, prefix_len):
    scale = 1.0 / math.sqrt(DH)

    def one_request(packed):
        req_q, req_kv, ident, owners, limit = packed
        rows_at = (owners * PAGES_DEV + ident).astype(jnp.int32)
        prefix = kv_store[rows_at].reshape(PREFIX, F)
        prefix_ok = jnp.arange(PREFIX) < limit
        every = jnp.concatenate([prefix, req_kv], 0)
        pairs = every.reshape(-1, 2, KVH, DH).astype(jnp.float32)
        key_rows = pairs[:, 0]
        val_rows = pairs[:, 1]

        def one_block(block):
            block_q, base = block
            q_four = block_q.reshape(QB, KVH, GROUP, DH).astype(jnp.float32)
            scores = jnp.einsum('qgjd,ngd->qgjn', q_four, key_rows, precision=lax.Precision.HIGHEST) * scale
            query_pos = base + jnp.arange(QB)
            span_ok = jnp.arange(SPAN)[None, :] <= query_pos[:, None]
            allowed = jnp.concatenate([jnp.broadcast_to(prefix_ok[None, :], (QB, PREFIX)), span_ok], 1)[:, None, None, :]
            row_top = lax.optimization_barrier(jnp.max(jnp.where(allowed, scores, -1e+30), axis=-1))
            weights = jnp.where(allowed, jnp.exp(scores - row_top[..., None]), 0.0)
            denom = lax.optimization_barrier(jnp.sum(weights, axis=-1))
            rounded = lax.optimization_barrier(weights.astype(jnp.bfloat16))
            numer = jnp.einsum('qgjn,ngd->qgjd', rounded.astype(jnp.float32), val_rows, precision=lax.Precision.HIGHEST)
            return (numer / denom[..., None]).astype(jnp.bfloat16).reshape(QB, QH * DH)
        starts = (jnp.arange(N_BLK) * QB).astype(jnp.int32)
        outputs = lax.map(one_block, (req_q.reshape(N_BLK, QB, QH * DH), starts))
        return outputs.reshape(SPAN, QH * DH)
    result = lax.map(one_request, (queries.reshape(N_POOL, SPAN, QH * DH), span_kv.reshape(N_POOL, SPAN, F), page_ids, page_owner, prefix_len))
    return result.reshape(TOKENS, QH * DH)
```

```python
import functools
import math

import jax
import jax.numpy as jnp
from jax import lax
from jax.experimental import pallas as pl
from jax.experimental.pallas import tpu as pltpu
from jax.sharding import PartitionSpec as P

KVH = 4
DH = 128
PAGE = 64
QB = 128
PAGES_DEV = 16
PAGES_REQ = 32
NY = 4
NZ = 8
NX = 4
CH = 4
CR = PAGE // CH
CK = PAGES_REQ * CR
SURE = 1280 // PAGE
RB = 256
ROWS = 1024
KC = 1024
BF = jnp.bfloat16
F32 = jnp.float32
MESH = pl.DeviceIdType.MESH
SCALE = math.log2(math.e) / math.sqrt(DH)
PLACE_OF = {0: 0, 1: 1, 7: 2, 2: 3, 6: 4, 3: 5, 5: 6, 4: 7}
GROUPS = {0: (0,), 1: (1, 7), 2: (2, 6), 3: (3, 5), 4: (4,)}


def dot(a, b, ca, cb):
    return lax.dot_general(a, b, (((ca,), (cb,)), ((), ())), preferred_element_type=F32)


def kernel(own_s, ids_s, len_s, own_v, q_hbm, span_hbm, store_hbm, out_ref, *scr):
    scr = list(scr)

    def take(n):
        got = scr[:n]
        del scr[:n]
        return got

    zb = [take(NZ) for _ in range(CH)]
    ysend = take(CH)
    rbuf = take(CH)
    (kvall, am, qraw, q2, acc, top, ltab, tab) = take(8)
    (loc_sem, tab_sem, list_ss, list_rs, z_ss, z_rs, y_ss, y_rs, x_ss, x_rs, p_ss, p_rs,
     sp_ss, sp_rs, spp_ss, spp_rs) = take(16)

    pool = lax.axis_index("pool")
    blk = lax.axis_index("blk")
    y, z = pool // NZ, pool % NZ
    x, c = blk // 2, blk % 2
    zr = (y * NZ + (z + 1) % NZ, blk)
    zl = (y * NZ + (z + NZ - 1) % NZ, blk)
    ydev = [(((y + d) % NY) * NZ + z, blk) for d in range(NY)]
    xdev = [(pool, ((x + d) % NX) * 2 + c) for d in range(NX)]
    mate = (pool, x * 2 + 1 - c)

    def rcopy(src, dst, ss, rs, dev):
        return pltpu.make_async_remote_copy(
            src_ref=src, dst_ref=dst, send_sem=ss, recv_sem=rs, device_id=dev, device_id_type=MESH)

    col = pl.multiple_of(c * (KVH * DH) + x * DH, DH)
    loads = []
    for h in range(CH):
        loads.append(pltpu.make_async_copy(
            store_hbm.at[:, pl.ds(h * CR, CR), pl.ds(col, DH)], zb[h][0], loc_sem.at[h]))
    for t in range(2):
        for g in range(KVH):
            loads.append(pltpu.make_async_copy(
                span_hbm.at[:, pl.ds((t * KVH + g) * DH, DH)], kvall.at[0, g, t, pl.ds(0, QB), :],
                loc_sem.at[4 + t * KVH + g]))
    loads.append(pltpu.make_async_copy(q_hbm, qraw, loc_sem.at[12]))
    for cp in loads:
        cp.start()
    barrier = pltpu.get_barrier_semaphore()
    near = [zr, zl] + ydev[1:] + xdev[1:] + [mate]
    for dev in near:
        pl.semaphore_signal(barrier, inc=1, device_id=dev, device_id_type=MESH)

    lane = lax.broadcasted_iota(jnp.int32, (8, 128), 1)
    row8 = lax.broadcasted_iota(jnp.int32, (8, 128), 0)
    owners_v = jnp.broadcast_to(own_v[...], (8, 128))
    seen = jnp.zeros((8, 128), jnp.int32)
    rank = jnp.zeros((8, 128), jnp.int32)
    page0 = jnp.zeros((8, 128), jnp.int32)
    page1 = jnp.zeros((8, 128), jnp.int32)
    for s in range(PAGES_REQ):
        o, ident = own_s[0, s], ids_s[0, s]
        hit = lane == o
        page0 = jnp.where(hit & (seen == 0), ident, page0)
        page1 = jnp.where(hit & (seen == 1), ident, page1)
        seen = seen + hit.astype(jnp.int32)
        rank = rank + ((owners_v == o) & (lane > s)).astype(jnp.int32)
    dd = ((owners_v >> 3) - y + NY) & (NY - 1)
    kk = (z - (owners_v & 7) + NZ) & (NZ - 1)
    jj = jnp.where(kk == 0, 0, jnp.where(kk < 4, 2 * kk - 1, jnp.where(kk == 4, 7, 2 * (8 - kk))))
    where_v = (dd * NZ + jj) * 2 + jnp.minimum(rank, 1)
    ltab[0] = jnp.where(row8 == 0, page0, jnp.where(row8 == 1, page1, where_v))

    limit = len_s[0]
    rowk = lax.broadcasted_iota(jnp.int32, (KC, DH), 0)
    am[0] = jnp.where(rowk // QB <= blk, 1.0, 0.0).astype(BF)
    for grp in range(2):
        within = rowk % CK
        pos = (within // CR) * PAGE + (grp * 2 + rowk // CK) * CR + within % CR
        am[1 + grp] = jnp.where(pos < limit, 1.0, 0.0).astype(BF)

    @pl.loop(0, KVH)
    def _(g):
        acc[g] = jnp.zeros((ROWS, 2 * DH), F32)
        top[g] = jnp.full((ROWS, DH), -1e30, F32)

    loads[12].wait()
    for hd in range(KVH * 8):
        qs = qraw[:, hd * DH:(hd + 1) * DH].astype(F32) * SCALE
        hi = qs.astype(BF)
        rows = pl.ds((hd % 8) * QB, QB)
        q2[hd // 8, rows, 0:DH] = hi
        q2[hd // 8, rows, DH:2 * DH] = (qs - hi.astype(F32)).astype(BF)
    for cp in loads[:12]:
        cp.wait()

    for j in range(1, 8):
        @pl.when(j > blk)
        def _():
            for g in range(KVH):
                first = kvall[0, g, 0, 0:1, :]
                kvall[0, g, 0, pl.ds(j * QB, QB), :] = jnp.broadcast_to(first, (QB, DH))
                kvall[0, g, 1, pl.ds(j * QB, QB), :] = jnp.zeros((QB, DH), BF)

    pl.semaphore_wait(barrier, len(near))

    def span_part(j):
        return kvall.at[0, :, :, pl.ds(pl.multiple_of(j * QB, QB), QB), :]

    def span_send(i):
        return rcopy(span_part(0), span_part(2 * i), sp_ss.at[i], sp_rs.at[i], xdev[i])

    def span_mate(i):
        return rcopy(span_part(2 * i), span_part(2 * i + 1 - 2 * c), spp_ss.at[i], spp_rs.at[i], mate)

    def span_start():
        for i in (1, 2, 3):
            @pl.when(x + i < NX)
            def _():
                span_send(i).start()

        @pl.when(c == 0)
        def _():
            span_mate(0).start()

    def span_pass(i):
        @pl.when(x >= i)
        def _():
            span_send(i).wait_recv()
            span_mate(i).start()

    def span_done():
        @pl.when(c == 1)
        def _():
            rcopy(span_part(0), span_part(1), spp_ss.at[0], spp_rs.at[0], mate).wait_recv()
        for i in (1, 2, 3):
            @pl.when(x >= i)
            def _():
                rcopy(span_part(2 * i), span_part(2 * i - 1 + 2 * c), spp_ss.at[i], spp_rs.at[i], mate).wait_recv()

    def list_send(d):
        return rcopy(ltab.at[0], ltab.at[d], list_ss.at[d], list_rs.at[d], ydev[d])

    HALF = PAGES_DEV // 2
    LO, HI = pl.ds(0, HALF), pl.ds(HALF, HALF)

    def z_up(h, k):
        if k < 3:
            return rcopy(zb[h][k], zb[h][k + 1], z_ss.at[h], z_rs.at[h, k + 1], zr)
        return rcopy(zb[h][3].at[LO], zb[h][4].at[LO], z_ss.at[h], z_rs.at[h, 4], zr)

    def z_down(h, k):
        src = (NZ - k) % NZ
        if k < 3:
            return rcopy(zb[h][src], zb[h][NZ - k - 1], z_ss.at[h], z_rs.at[h, NZ - k - 1], zl)
        return rcopy(zb[h][5].at[HI], zb[h][4].at[HI], z_ss.at[h], z_rs.at[h, 0], zl)

    def y_send(h, e, d):
        lo = 0 if e == 0 else 2 * (2 * e - 1)
        part = pl.ds(lo, 2 * len(GROUPS[e]))
        return rcopy(ysend[h].at[d, part], rbuf[h].at[d, part], y_ss.at[h], y_rs.at[h], ydev[(NY - d) % NY])

    def pack(h, e):
        for k in GROUPS[e]:
            j = PLACE_OF[k]
            owner = y * NZ + (z + NZ - k) % NZ
            for d in range(NY):
                for slot in range(2):
                    page = tab[d, slot, owner]
                    dst = rbuf[h].at[0] if d == 0 else ysend[h].at[d]
                    dst[2 * j + slot] = zb[h][k][page]
        for d in range(1, NY):
            y_send(h, e, d).start()

    def own(h):
        z_up(h, 0).start()
        z_down(h, 0).start()

    def ring(h, k):
        z_up(h, k - 1).wait_recv()
        if k < 4:
            z_up(h, k).start()
        z_down(h, k - 1).wait_recv()
        if k < 4:
            z_down(h, k).start()
        pack(h, k)

    def part(h, r):
        g = (x + NX - r) % NX
        return lambda t, half=None: kvall.at[
            1 + h // 2, g, t,
            pl.ds((h % 2) * CK + (0 if half is None else half * (CK // 2)), CK if half is None else CK // 2), :]

    def x_send(h, up):
        mine = part(h, 0)(c)
        return rcopy(mine, mine, x_ss.at[h], x_rs.at[h, 0 if up else 1], xdev[1] if up else xdev[3])

    def x_recv(h, up):
        got = part(h, 1 if up else 3)(c)
        return rcopy(got, got, x_ss.at[h], x_rs.at[h, 0 if up else 1], xdev[1])

    def x_pass(h, up):
        got = part(h, 1 if up else 3)(c, 0 if up else 1)
        return rcopy(got, got, x_ss.at[h], x_rs.at[h, 2 if up else 3], xdev[1] if up else xdev[3])

    def x_far(h, up):
        got = part(h, 2)(c, 0 if up else 1)
        return rcopy(got, got, x_ss.at[h], x_rs.at[h, 2 if up else 3], xdev[1])

    def m_send(h, r):
        mine = part(h, r)(c)
        return rcopy(mine, mine, p_ss.at[h], p_rs.at[h, r], mate)

    def m_recv(h, r):
        got = part(h, r)(1 - c)
        return rcopy(got, got, p_ss.at[h], p_rs.at[h, r], mate)

    def compact(h):
        whole = rbuf[h].at[pl.ds(1, NY - 1)]
        rcopy(whole, whole, y_ss.at[h], y_rs.at[h], mate).wait_recv()
        grp, base = 1 + h // 2, (h % 2) * CK
        rows = lax.broadcasted_iota(jnp.int32, (CR, DH), 0)
        fill = None
        for s in range(PAGES_REQ):
            at = tab[0, 2, s]
            page = rbuf[h][at // 16, at % 16]
            if s == 0:
                fill = jnp.broadcast_to(page[0:1].astype(F32), (CR, DH)) * (1 - c).astype(F32)
            if s >= SURE:
                page = jnp.where(rows < limit - (s * PAGE + h * CR), page.astype(F32), fill).astype(BF)
            kvall[grp, x, c, pl.ds(base + s * CR, CR), :] = page
        x_send(h, True).start()
        x_send(h, False).start()
        m_send(h, 0).start()

    def neighbours(h):
        x_recv(h, True).wait_recv()
        x_pass(h, True).start()
        x_recv(h, False).wait_recv()
        x_pass(h, False).start()
        m_send(h, 1).start()
        m_send(h, 3).start()

    def opposite(h):
        x_far(h, True).wait_recv()
        x_far(h, False).wait_recv()
        m_send(h, 2).start()

    for i in (1, 2, 3):
        list_send(i).start()
    own(0)
    span_start()
    own(1)
    for i in (1, 2, 3):
        list_send(i).wait_recv()
    cp = pltpu.make_async_copy(ltab, tab, tab_sem.at[0])
    cp.start()
    cp.wait()
    for h in range(CH):
        pack(h, 0)

    def E(h, k): return lambda: ring(h, k)
    def O(h): return lambda: own(h)
    def C(h): return lambda: compact(h)
    def N(h): return lambda: neighbours(h)
    def F(h): return lambda: opposite(h)
    def SP(i): return lambda: span_pass(i)

    plan = PLAN(E, O, C, N, F, SP, span_done)
    for step in plan[-1]:
        step()

    @pl.loop(0, 12)
    def _(u):
        grp = u // 4
        i = u % 4
        r = i + i // 2 - 2 * (i // 3)
        g = (x + NX - r) % NX

        def hook(place):
            for at, steps in plan.items():
                if at >= 0 and at % 4 == place:
                    @pl.when(u == at // 4)
                    def _():
                        for step in steps:
                            step()

        hook(0)
        for uu in range(4, 12):
            @pl.when(u == uu)
            def _():
                rr = (0, 1, 3, 2)[uu % 4]
                for h in (0, 1):
                    m_recv((uu // 4 - 1) * 2 + h, rr).wait_recv()
        keys = kvall[grp, g, 0]
        vals = kvall[grp, g, 1]
        k2 = jnp.concatenate([keys, keys], axis=1)
        v2 = jnp.concatenate([vals, am[grp]], axis=1)
        token = lax.broadcasted_iota(jnp.int32, (RB, QB), 0) % QB
        key = lax.broadcasted_iota(jnp.int32, (RB, QB), 1)
        inside = (key <= token) | (grp > 0)

        def scores(rb):
            s = dot(q2[g, pl.ds(rb * RB, RB), :], k2, 1, 1)
            return jnp.concatenate([jnp.where(inside, s[:, :QB], -1e30), s[:, QB:]], axis=1)

        def granule(rb, s):
            rows = pl.ds(rb * RB, RB)
            old = top[g, rows, 0:1]
            new = jnp.maximum(old, jnp.max(s, axis=1, keepdims=True))
            p = jnp.exp2(s - new).astype(BF)
            acc[g, rows, :] = acc[g, rows, :] * jnp.exp2(old - new) + dot(p, v2, 1, 0)
            top[g, rows, :] = jnp.broadcast_to(new, (RB, DH))

        n = ROWS // RB
        for pair in range(n // 2):
            if pair:
                hook(pair * 2)
            s0 = scores(2 * pair)
            s1 = scores(2 * pair + 1)
            granule(2 * pair, s0)
            granule(2 * pair + 1, s1)

        @pl.when(grp == 2)
        def _():
            for hd in range(8):
                a = acc[g, pl.ds(hd * QB, QB), :]
                out_ref[:, pl.ds(pl.multiple_of((g * 8 + hd) * DH, DH), DH)] = (
                    a[:, :DH] / a[:, DH:]).astype(BF)

    for i in (1, 2, 3):
        list_send(i).wait_send()

        @pl.when(x + i < NX)
        def _():
            span_send(i).wait_send()

        @pl.when(x >= i)
        def _():
            span_mate(i).wait_send()

    @pl.when(c == 0)
    def _():
        span_mate(0).wait_send()
    for h in range(CH):
        for ref, ss in (
            (kvall.at[1, pl.ds(0, 3), 0, pl.ds(0, CK), :], x_ss.at[h]),
            (kvall.at[1, :, 0, pl.ds(0, CK), :], p_ss.at[h]),
            (ysend[h].at[pl.ds(1, NY - 1)], y_ss.at[h]),
        ):
            rcopy(ref, ref, ss, ss, mate).wait_send()
        z_wait = kvall.at[1, 0, :, pl.ds(0, 7 * PAGES_DEV * CR // 2), :]
        rcopy(z_wait, z_wait, z_ss.at[h], z_ss.at[h], mate).wait_send()


def PLAN(E, O, C, N, F, SP, SD):
    return {
        -1: [E(0, 1), E(0, 2), E(1, 1), E(0, 3), O(2), E(1, 2), SP(1), E(0, 4), E(1, 3), C(0), SP(3), E(2, 1), SP(2), SD],
        0: [E(1, 4), O(3), E(2, 2)],
        2: [C(1), E(3, 1), E(2, 3)],
        4: [N(0)],
        6: [E(3, 2), E(2, 4)],
        8: [C(2), E(3, 3), F(0)],
        10: [N(1)],
        14: [E(3, 4), F(1)],
        16: [C(3)],
        18: [N(2)],
        22: [F(2)],
        28: [N(3)],
        36: [F(3)],
    }


def per_device(queries, span_kv, kv_store, page_ids, page_owner, prefix_len):
    anyw = pl.BlockSpec(memory_space=pl.ANY)
    smem = pl.BlockSpec(memory_space=pltpu.SMEM)
    vmem = pl.BlockSpec(memory_space=pltpu.VMEM)
    dma = pltpu.SemaphoreType.DMA
    owners_row = jnp.pad(page_owner, ((0, 0), (0, 128 - PAGES_REQ)))
    scratch = [pltpu.VMEM((PAGES_DEV, CR, DH), BF) for _ in range(CH * NZ)]
    scratch += [pltpu.VMEM((NY, 2 * NZ, CR, DH), BF) for _ in range(2 * CH)]
    scratch += [
        pltpu.VMEM((3, KVH, 2, KC, DH), BF),
        pltpu.VMEM((3, KC, DH), BF),
        pltpu.VMEM((QB, KVH * 8 * DH), BF),
        pltpu.VMEM((KVH, ROWS, 2 * DH), BF),
        pltpu.VMEM((KVH, ROWS, 2 * DH), F32),
        pltpu.VMEM((KVH, ROWS, DH), F32),
        pltpu.VMEM((NY, 8, 128), jnp.int32),
        pltpu.SMEM((NY, 8, 128), jnp.int32),
        dma((13,)), dma((1,)), dma((4,)), dma((4,)),
        dma((CH,)), dma((CH, NZ)),
        dma((CH,)), dma((CH,)),
        dma((CH,)), dma((CH, 4)),
        dma((CH,)), dma((CH, 4)),
        dma((4,)), dma((4,)), dma((4,)), dma((4,)),
    ]
    return pl.pallas_call(
        kernel,
        out_shape=jax.ShapeDtypeStruct(queries.shape, BF),
        in_specs=[smem, smem, smem, vmem, anyw, anyw, anyw],
        out_specs=vmem,
        scratch_shapes=scratch,
        compiler_params=pltpu.CompilerParams(
            vmem_limit_bytes=56 * 2**20, collective_id=0, has_side_effects=True),
        cost_estimate=pl.CostEstimate(
            flops=4 * 4096 * 3072 * 128, bytes_accessed=4 * 2**20, transcendentals=4096 * 3072),
    )(page_owner, page_ids, prefix_len, owners_row, queries, span_kv, kv_store)


def solution(mesh):
    in_specs = (
        P(("pool", "blk"), None),
        P(("pool", "blk"), None),
        P("pool", None, None),
        P("pool", None),
        P("pool", None),
        P("pool"),
    )
    return jax.shard_map(
        per_device, mesh=mesh, in_specs=in_specs, out_specs=P(("pool", "blk"), None), check_vma=False
    )
```

```python
import functools
import math

import jax
import jax.numpy as jnp
from jax import lax
from jax.experimental import pallas as pl
from jax.experimental.pallas import tpu as pltpu
from jax.sharding import PartitionSpec as P

KVH = 4
DH = 128
PAGE = 64
QB = 128
PAGES_DEV = 16
PAGES_REQ = 32
NY = 4
NZ = 8
NX = 4
CH = 4
CR = PAGE // CH
CK = PAGES_REQ * CR
SURE = 1280 // PAGE
RB = 256
ROWS = 1024
KC = 1024
BF = jnp.bfloat16
F32 = jnp.float32
MESH = pl.DeviceIdType.MESH
SCALE = math.log2(math.e) / math.sqrt(DH)
PLACE_OF = {0: 0, 1: 1, 7: 2, 2: 3, 6: 4, 3: 5, 5: 6, 4: 7}
GROUPS = {0: (0,), 1: (1, 7), 2: (2, 6)}
NEAR = 10
FAR = 6
COLS = (0, 1, -1, 2, -2)
FAR_SLOTS = ((2, 1, 0), (2, 1, 1), (6, 2, 0), (6, 2, 1), (2, 3, 0), (6, 4, 1))
FAR_RUNS = ((0, 2, 1), (2, 2, 2), (4, 1, 3), (5, 1, 4))


def dot(a, b, ca, cb):
    return lax.dot_general(a, b, (((ca,), (cb,)), ((), ())), preferred_element_type=F32)


def kernel(own_s, ids_s, len_s, own_v, q_hbm, span_hbm, store_hbm, out_ref, *scr):
    scr = list(scr)

    def take(n):
        got = scr[:n]
        del scr[:n]
        return got

    zb = [dict(zip((0, 1, 2, 6, 7), take(5))) for _ in range(CH)]
    ysend = take(CH)
    fsend = take(CH)
    rbuf = take(CH)
    (kvall, am, qraw, q2, acc, top, ltab, tab, wtab, wtab_s) = take(10)
    (loc_sem, tab_sem, list_ss, list_rs, z_ss, z_rs, y_ss, y_rs, f_ss, f_rs, x_ss, x_rs, p_ss, p_rs,
     sp_ss, sp_rs, spp_ss, spp_rs) = take(18)

    pool = lax.axis_index("pool")
    blk = lax.axis_index("blk")
    y, z = pool // NZ, pool % NZ
    x, c = blk // 2, blk % 2
    zr = (y * NZ + (z + 1) % NZ, blk)
    zl = (y * NZ + (z + NZ - 1) % NZ, blk)
    ydev = [(((y + d) % NY) * NZ + z, blk) for d in range(NY)]
    xdev = [(pool, ((x + d) % NX) * 2 + c) for d in range(NX)]
    mate = (pool, x * 2 + 1 - c)

    def rcopy(src, dst, ss, rs, dev):
        return pltpu.make_async_remote_copy(
            src_ref=src, dst_ref=dst, send_sem=ss, recv_sem=rs, device_id=dev, device_id_type=MESH)

    col = pl.multiple_of(c * (KVH * DH) + x * DH, DH)
    loads = []
    for h in range(CH):
        loads.append(pltpu.make_async_copy(
            store_hbm.at[:, pl.ds(h * CR, CR), pl.ds(col, DH)], zb[h][0], loc_sem.at[h]))
    for t in range(2):
        for g in range(KVH):
            loads.append(pltpu.make_async_copy(
                span_hbm.at[:, pl.ds((t * KVH + g) * DH, DH)], kvall.at[0, g, t, pl.ds(0, QB), :],
                loc_sem.at[4 + t * KVH + g]))
    loads.append(pltpu.make_async_copy(q_hbm, qraw, loc_sem.at[12]))
    for cp in loads:
        cp.start()
    barrier = pltpu.get_barrier_semaphore()
    def at(dz, d):
        return (((y + d) % NY) * NZ + (z + NZ + dz) % NZ, blk)

    near = [at(dz, d) for dz in COLS for d in range(NY) if dz or d] + xdev[1:] + [mate]
    for dev in near:
        pl.semaphore_signal(barrier, inc=1, device_id=dev, device_id_type=MESH)

    shape = (8, PAGES_REQ)
    lane = lax.broadcasted_iota(jnp.int32, shape, 1)
    row8 = lax.broadcasted_iota(jnp.int32, shape, 0)
    owners_v = jnp.broadcast_to(own_v[...], shape)
    seen = jnp.zeros(shape, jnp.int32)
    rank = jnp.zeros(shape, jnp.int32)
    page0 = jnp.zeros(shape, jnp.int32)
    page1 = jnp.zeros(shape, jnp.int32)
    for s in range(PAGES_REQ):
        o, ident = own_s[0, s], ids_s[0, s]
        hit = lane == o
        page0 = jnp.where(hit & (seen == 0), ident, page0)
        page1 = jnp.where(hit & (seen == 1), ident, page1)
        seen = seen + hit.astype(jnp.int32)
        rank = rank + ((owners_v == o) & (lane > s)).astype(jnp.int32)
    dd = ((owners_v >> 3) - y + NY) & (NY - 1)
    kk = (z - (owners_v & 7) + NZ) & (NZ - 1)
    jj = jnp.where(kk == 0, 0, jnp.where(kk < 4, 2 * kk - 1, jnp.where(kk == 4, 7, 2 * (8 - kk))))
    where_v = (dd * NZ + jj) * 2 + jnp.minimum(rank, 1)
    table = jnp.where(row8 == 0, page0 + PAGES_DEV * page1, where_v)
    ltab[0, 0] = jnp.zeros((1, 128), jnp.int32)
    ltab[0, 0, :, 0:PAGES_REQ] = table[0:1]
    wtab[...] = jnp.zeros((1, 128), jnp.int32)
    wtab[:, 0:PAGES_REQ] = table[1:2]

    limit = len_s[0]
    for cp in loads[:12]:
        cp.wait()
    pl.semaphore_wait(barrier, len(near))

    def prepare():
        rowk = lax.broadcasted_iota(jnp.int32, (KC, DH), 0)
        am[0] = jnp.where(rowk // QB <= blk, 1.0, 0.0).astype(BF)
        for grp in range(2):
            within = rowk % CK
            pos = (within // CR) * PAGE + (grp * 2 + rowk // CK) * CR + within % CR
            am[1 + grp] = jnp.where(pos < limit, 1.0, 0.0).astype(BF)

        @pl.loop(0, KVH)
        def _(g):
            acc[g] = jnp.zeros((ROWS, 2 * DH), F32)
            top[g] = jnp.full((ROWS, DH), -1e30, F32)

        loads[12].wait()
        for hd in range(KVH * 8):
            qs = qraw[:, hd * DH:(hd + 1) * DH].astype(F32) * SCALE
            hi = qs.astype(BF)
            rows = pl.ds((hd % 8) * QB, QB)
            q2[hd // 8, rows, 0:DH] = hi
            q2[hd // 8, rows, DH:2 * DH] = (qs - hi.astype(F32)).astype(BF)
        for j in range(1, 8):
            @pl.when(j > blk)
            def _():
                for g in range(KVH):
                    first = kvall[0, g, 0, 0:1, :]
                    kvall[0, g, 0, pl.ds(j * QB, QB), :] = jnp.broadcast_to(first, (QB, DH))
                    kvall[0, g, 1, pl.ds(j * QB, QB), :] = jnp.zeros((QB, DH), BF)

    def span_part(j):
        return kvall.at[0, :, :, pl.ds(pl.multiple_of(j * QB, QB), QB), :]

    def span_send(i):
        return rcopy(span_part(0), span_part(2 * i), sp_ss.at[i], sp_rs.at[i], xdev[i])

    def span_mate(i):
        return rcopy(span_part(2 * i), span_part(2 * i + 1 - 2 * c), spp_ss.at[i], spp_rs.at[i], mate)

    def span_start():
        for i in (1, 2, 3):
            @pl.when(x + i < NX)
            def _():
                span_send(i).start()

        @pl.when(c == 0)
        def _():
            span_mate(0).start()

    def span_pass(i):
        @pl.when(x >= i)
        def _():
            span_send(i).wait_recv()
            span_mate(i).start()

    def span_done():
        @pl.when(c == 1)
        def _():
            rcopy(span_part(0), span_part(1), spp_ss.at[0], spp_rs.at[0], mate).wait_recv()
        for i in (1, 2, 3):
            @pl.when(x >= i)
            def _():
                rcopy(span_part(2 * i), span_part(2 * i - 1 + 2 * c), spp_ss.at[i], spp_rs.at[i], mate).wait_recv()

    def list_send(col, d):
        ss, rs = (list_ss.at[0], list_rs.at[0]) if col == 0 else (list_ss.at[1], list_rs.at[1])
        return rcopy(ltab.at[0, 0], ltab.at[col, d], ss, rs, at(-COLS[col], d))

    def lists_start():
        for col in range(len(COLS)):
            for d in range(NY):
                if col or d:
                    list_send(col, d).start()

    def lists_wait(recv):
        for i, part in ((0, ltab.at[0, pl.ds(1, NY - 1)]), (1, ltab.at[pl.ds(1, 4)])):
            cp = rcopy(part, part, list_ss.at[i], list_rs.at[i], mate)
            if recv:
                cp.wait_recv()
            else:
                cp.wait_send()

    def tables():
        lists_wait(True)
        cps = [pltpu.make_async_copy(ltab, tab, tab_sem.at[0]), pltpu.make_async_copy(wtab, wtab_s, tab_sem.at[1])]
        for cp in cps:
            cp.start()
        for cp in cps:
            cp.wait()

    def z_up(h, k):
        return rcopy(zb[h][k], zb[h][k + 1], z_ss.at[h], z_rs.at[h, k + 1], zr)

    def z_down(h, k):
        return rcopy(zb[h][(NZ - k) % NZ], zb[h][NZ - k - 1], z_ss.at[h], z_rs.at[h, NZ - k - 1], zl)

    def y_send(h, e, d):
        lo = 0 if e == 0 else 2 * (2 * e - 1)
        part = pl.ds(lo, 2 * len(GROUPS[e]))
        return rcopy(ysend[h].at[d, part], rbuf[h].at[d, part], y_ss.at[h], y_rs.at[h], at(0, NY - d))

    def f_send(h, lo, n, col, d):
        return rcopy(fsend[h].at[d, pl.ds(lo, n)], rbuf[h].at[d, pl.ds(NEAR + lo, n)], f_ss.at[h], f_rs.at[h],
                     at(COLS[col], NY - d))

    def pack(h, e):
        pages = {}
        for k in GROUPS[e]:
            owner = y * NZ + (z + NZ - k) % NZ
            for d in range(NY):
                for slot in range(2):
                    both = tab[0, d, 0, owner]
                    pages[k, d, slot] = both >> 4 if slot else both & 15
        got = {key: zb[h][key[0]][page] for key, page in pages.items()}
        for (k, d, slot), value in got.items():
            dst = rbuf[h].at[0] if d == 0 else ysend[h].at[d]
            dst[2 * PLACE_OF[k] + slot] = value
        for d in range(1, NY):
            y_send(h, e, d).start()

    def pack_far(h):
        pages = {}
        for d in range(NY):
            for i, (k, col, slot) in enumerate(FAR_SLOTS):
                both = tab[col, d, 0, y * NZ + (z + NZ - k) % NZ]
                pages[d, i] = both >> 4 if slot else both & 15
        got = {key: zb[h][FAR_SLOTS[key[1]][0]][page] for key, page in pages.items()}
        for (d, i), value in got.items():
            fsend[h][d, i] = value
        for lo, n, col in FAR_RUNS:
            for d in range(NY):
                f_send(h, lo, n, col, d).start()

    def own(h):
        z_up(h, 0).start()
        z_down(h, 0).start()

    def ring(h, k):
        z_up(h, k - 1).wait_recv()
        if k == 1:
            z_up(h, 1).start()
        z_down(h, k - 1).wait_recv()
        if k == 1:
            z_down(h, 1).start()

    def part(h, r):
        g = (x + NX - r) % NX
        return lambda t, half=None: kvall.at[
            1 + h // 2, g, t,
            pl.ds((h % 2) * CK + (0 if half is None else half * (CK // 2)), CK if half is None else CK // 2), :]

    def x_send(h, up):
        mine = part(h, 0)(c)
        return rcopy(mine, mine, x_ss.at[h], x_rs.at[h, 0 if up else 1], xdev[1] if up else xdev[3])

    def x_recv(h, up):
        got = part(h, 1 if up else 3)(c)
        return rcopy(got, got, x_ss.at[h], x_rs.at[h, 0 if up else 1], xdev[1])

    def x_pass(h, up):
        got = part(h, 1 if up else 3)(c, 0 if up else 1)
        return rcopy(got, got, x_ss.at[h], x_rs.at[h, 2 if up else 3], xdev[1] if up else xdev[3])

    def x_far(h, up):
        got = part(h, 2)(c, 0 if up else 1)
        return rcopy(got, got, x_ss.at[h], x_rs.at[h, 2 if up else 3], xdev[1])

    def m_send(h, r):
        mine = part(h, r)(c)
        return rcopy(mine, mine, p_ss.at[h], p_rs.at[h, r], mate)

    def m_recv(h, r):
        got = part(h, r)(1 - c)
        return rcopy(got, got, p_ss.at[h], p_rs.at[h, r], mate)

    def compact(h):
        part_in = rbuf[h].at[pl.ds(1, NY - 1), pl.ds(0, NEAR)]
        rcopy(part_in, part_in, y_ss.at[h], y_rs.at[h], mate).wait_recv()
        part_in = rbuf[h].at[:, pl.ds(NEAR, FAR)]
        rcopy(part_in, part_in, f_ss.at[h], f_rs.at[h], mate).wait_recv()
        grp, base = 1 + h // 2, (h % 2) * CK
        rows = lax.broadcasted_iota(jnp.int32, (CR, DH), 0)
        fill = None
        places = [wtab_s[0, s] for s in range(PAGES_REQ)]
        pages = [rbuf[h][place >> 4, place & 15] for place in places]
        for s, page in enumerate(pages):
            if s == 0:
                fill = jnp.broadcast_to(page[0:1].astype(F32), (CR, DH)) * (1 - c).astype(F32)
            if s >= SURE:
                page = jnp.where(rows < limit - (s * PAGE + h * CR), page.astype(F32), fill).astype(BF)
            kvall[grp, x, c, pl.ds(base + s * CR, CR), :] = page
        x_send(h, True).start()
        x_send(h, False).start()
        m_send(h, 0).start()

    def neighbours(h):
        x_recv(h, True).wait_recv()
        x_pass(h, True).start()
        x_recv(h, False).wait_recv()
        x_pass(h, False).start()
        m_send(h, 1).start()
        m_send(h, 3).start()

    def opposite(h):
        x_far(h, True).wait_recv()
        x_far(h, False).wait_recv()
        m_send(h, 2).start()

    def R(h, k): return lambda: ring(h, k)
    def Q(h, e): return lambda: pack(h, e)
    def Z(h): return lambda: pack_far(h)
    def O(h): return lambda: own(h)
    def C(h): return lambda: compact(h)
    def N(h): return lambda: neighbours(h)
    def F(h): return lambda: opposite(h)
    def SP(i): return lambda: span_pass(i)

    plan = PLAN(R, Q, Z, O, C, N, F, SP, span_done, lists_start, span_start, tables, prepare)
    for step in plan[-1]:
        step()

    @pl.loop(0, 12)
    def _(u):
        grp = u // 4
        i = u % 4
        r = i + i // 2 - 2 * (i // 3)
        g = (x + NX - r) % NX

        def hook(place):
            for at, steps in plan.items():
                if at >= 0 and at % 4 == place:
                    @pl.when(u == at // 4)
                    def _():
                        for step in steps:
                            step()

        hook(0)
        for uu in range(4, 12):
            @pl.when(u == uu)
            def _():
                rr = (0, 1, 3, 2)[uu % 4]
                for h in (0, 1):
                    m_recv((uu // 4 - 1) * 2 + h, rr).wait_recv()
        keys = kvall[grp, g, 0]
        vals = kvall[grp, g, 1]
        k2 = jnp.concatenate([keys, keys], axis=1)
        v2 = jnp.concatenate([vals, am[grp]], axis=1)
        token = lax.broadcasted_iota(jnp.int32, (RB, QB), 0) % QB
        key = lax.broadcasted_iota(jnp.int32, (RB, QB), 1)
        inside = (key <= token) | (grp > 0)

        def scores(rb):
            s = dot(q2[g, pl.ds(rb * RB, RB), :], k2, 1, 1)
            return jnp.concatenate([jnp.where(inside, s[:, :QB], -1e30), s[:, QB:]], axis=1)

        def granule(rb, s):
            rows = pl.ds(rb * RB, RB)
            old = top[g, rows, 0:1]
            new = jnp.maximum(old, jnp.max(s, axis=1, keepdims=True))
            p = jnp.exp2(s - new).astype(BF)
            acc[g, rows, :] = acc[g, rows, :] * jnp.exp2(old - new) + dot(p, v2, 1, 0)
            top[g, rows, :] = jnp.broadcast_to(new, (RB, DH))

        n = ROWS // RB
        for pair in range(n // 2):
            if pair:
                hook(pair * 2)
            s0 = scores(2 * pair)
            s1 = scores(2 * pair + 1)
            granule(2 * pair, s0)
            granule(2 * pair + 1, s1)

        @pl.when(grp == 2)
        def _():
            for hd in range(8):
                a = acc[g, pl.ds(hd * QB, QB), :]
                out_ref[:, pl.ds(pl.multiple_of((g * 8 + hd) * DH, DH), DH)] = (
                    a[:, :DH] / a[:, DH:]).astype(BF)

    lists_wait(False)
    for i in (1, 2, 3):
        @pl.when(x + i < NX)
        def _():
            span_send(i).wait_send()

        @pl.when(x >= i)
        def _():
            span_mate(i).wait_send()

    @pl.when(c == 0)
    def _():
        span_mate(0).wait_send()
    for h in range(CH):
        for ref, ss in (
            (kvall.at[1, pl.ds(0, 3), 0, pl.ds(0, CK), :], x_ss.at[h]),
            (kvall.at[1, :, 0, pl.ds(0, CK), :], p_ss.at[h]),
            (ysend[h].at[pl.ds(1, NY - 1)], y_ss.at[h]),
            (fsend[h], f_ss.at[h]),
        ):
            rcopy(ref, ref, ss, ss, mate).wait_send()
        z_wait = kvall.at[1, 0, 0, pl.ds(0, 4 * PAGES_DEV * CR), :]
        rcopy(z_wait, z_wait, z_ss.at[h], z_ss.at[h], mate).wait_send()


def PLAN(R, Q, Z, O, C, N, F, SP, SD, LS, SS, LT, PR):
    return {
        -1: [O(0), LS, SS, O(1), PR, R(0, 1), LT, O(2), Q(0, 0), Q(0, 1), R(1, 1), O(3), R(0, 2), Q(0, 2), Z(0), Q(1, 0), Q(1, 1), R(2, 1), Q(2, 0), Q(2, 1), R(1, 2), Q(1, 2), Z(1), R(3, 1), Q(3, 0), Q(3, 1), SP(1), SP(3), SP(2), C(0), R(2, 2), Q(2, 2), Z(2), SD],
        0: [R(3, 2), Q(3, 2), Z(3)],
        4: [C(1)],
        8: [N(0)],
        12: [C(2)],
        16: [N(1), F(0)],
        20: [C(3)],
        24: [N(2), F(1)],
        30: [N(3), F(2)],
        38: [F(3)],
    }


def per_device(queries, span_kv, kv_store, page_ids, page_owner, prefix_len):
    anyw = pl.BlockSpec(memory_space=pl.ANY)
    smem = pl.BlockSpec(memory_space=pltpu.SMEM)
    vmem = pl.BlockSpec(memory_space=pltpu.VMEM)
    dma = pltpu.SemaphoreType.DMA
    scratch = [pltpu.VMEM((PAGES_DEV, CR, DH), BF) for _ in range(CH * 5)]
    scratch += [pltpu.VMEM((NY, NEAR, CR, DH), BF) for _ in range(CH)]
    scratch += [pltpu.VMEM((NY, FAR, CR, DH), BF) for _ in range(CH)]
    scratch += [pltpu.VMEM((NY, NEAR + FAR, CR, DH), BF) for _ in range(CH)]
    scratch += [
        pltpu.VMEM((3, KVH, 2, KC, DH), BF),
        pltpu.VMEM((3, KC, DH), BF),
        pltpu.VMEM((QB, KVH * 8 * DH), BF),
        pltpu.VMEM((KVH, ROWS, 2 * DH), BF),
        pltpu.VMEM((KVH, ROWS, 2 * DH), F32),
        pltpu.VMEM((KVH, ROWS, DH), F32),
        pltpu.VMEM((len(COLS), NY, 1, 128), jnp.int32),
        pltpu.SMEM((len(COLS), NY, 1, 128), jnp.int32),
        pltpu.VMEM((1, 128), jnp.int32),
        pltpu.SMEM((1, 128), jnp.int32),
        dma((13,)), dma((2,)), dma((2,)), dma((2,)),
        dma((CH,)), dma((CH, NZ)),
        dma((CH,)), dma((CH,)), dma((CH,)), dma((CH,)),
        dma((CH,)), dma((CH, 4)),
        dma((CH,)), dma((CH, 4)),
        dma((4,)), dma((4,)), dma((4,)), dma((4,)),
    ]
    return pl.pallas_call(
        kernel,
        out_shape=jax.ShapeDtypeStruct(queries.shape, BF),
        in_specs=[smem, smem, smem, vmem, anyw, anyw, anyw],
        out_specs=vmem,
        scratch_shapes=scratch,
        compiler_params=pltpu.CompilerParams(
            vmem_limit_bytes=56 * 2**20, collective_id=0, has_side_effects=True),
        cost_estimate=pl.CostEstimate(
            flops=4 * 4096 * 3072 * 128, bytes_accessed=4 * 2**20, transcendentals=4096 * 3072),
    )(page_owner, page_ids, prefix_len, page_owner, queries, span_kv, kv_store)


def solution(mesh):
    in_specs = (
        P(("pool", "blk"), None),
        P(("pool", "blk"), None),
        P("pool", None, None),
        P("pool", None),
        P("pool", None),
        P("pool"),
    )
    return jax.shard_map(
        per_device, mesh=mesh, in_specs=in_specs, out_specs=P(("pool", "blk"), None), check_vma=False
    )
```

```python
import functools
import math

import jax
import jax.numpy as jnp
from jax import lax
from jax.experimental import pallas as pl
from jax.experimental.pallas import tpu as pltpu
from jax.sharding import PartitionSpec as P

KVH = 4
DH = 128
PAGE = 64
QB = 128
PAGES_DEV = 16
PAGES_REQ = 32
NY = 4
NZ = 8
NX = 4
CH = 4
CR = PAGE // CH
CK = PAGES_REQ * CR
SURE = 1280 // PAGE
RB = 256
ROWS = 1024
KC = 1024
BF = jnp.bfloat16
F32 = jnp.float32
MESH = pl.DeviceIdType.MESH
SCALE = math.log2(math.e) / math.sqrt(DH)
PLACE_OF = {0: 0, 1: 1, 7: 2, 2: 3, 6: 4, 3: 5, 5: 6, 4: 7}
GROUPS = {0: (0,), 1: (1, 7), 2: (2, 6)}
NEAR = 10
FAR = 6
COLS = (0, 1, -1, 2, -2)
FAR_SLOTS = ((2, 1, 0), (2, 1, 1), (6, 2, 0), (6, 2, 1), (2, 3, 0), (6, 4, 1))
FAR_RUNS = ((0, 2, 1), (2, 2, 2), (4, 1, 3), (5, 1, 4))


def dot(a, b, ca, cb):
    return lax.dot_general(a, b, (((ca,), (cb,)), ((), ())), preferred_element_type=F32)


def kernel(own_s, ids_s, len_s, own_v, q_hbm, span_hbm, store_hbm, out_ref, *scr):
    scr = list(scr)

    def take(n):
        got = scr[:n]
        del scr[:n]
        return got

    zb = [dict(zip((0, 1, 2, 6, 7), take(5))) for _ in range(CH)]
    ysend = take(CH)
    fsend = take(CH)
    rbuf = take(CH)
    (kvall, am, qraw, q2, acc, top, ltab, tab, wtab, wtab_s) = take(10)
    (loc_sem, tab_sem, list_ss, list_rs, z_ss, z_rs, y_ss, y_rs, f_ss, f_rs, x_ss, x_rs, p_ss, p_rs,
     sp_ss, sp_rs, spp_ss, spp_rs) = take(18)

    pool = lax.axis_index("pool")
    blk = lax.axis_index("blk")
    y, z = pool // NZ, pool % NZ
    x, c = blk // 2, blk % 2
    zr = (y * NZ + (z + 1) % NZ, blk)
    zl = (y * NZ + (z + NZ - 1) % NZ, blk)
    ydev = [(((y + d) % NY) * NZ + z, blk) for d in range(NY)]
    xdev = [(pool, ((x + d) % NX) * 2 + c) for d in range(NX)]
    mate = (pool, x * 2 + 1 - c)

    def rcopy(src, dst, ss, rs, dev):
        return pltpu.make_async_remote_copy(
            src_ref=src, dst_ref=dst, send_sem=ss, recv_sem=rs, device_id=dev, device_id_type=MESH)

    col = pl.multiple_of(c * (KVH * DH) + x * DH, DH)
    loads = []
    for h in range(CH):
        loads.append(pltpu.make_async_copy(
            store_hbm.at[:, pl.ds(h * CR, CR), pl.ds(col, DH)], zb[h][0], loc_sem.at[h]))
    for t in range(2):
        for g in range(KVH):
            loads.append(pltpu.make_async_copy(
                span_hbm.at[:, pl.ds((t * KVH + g) * DH, DH)], kvall.at[0, g, t, pl.ds(0, QB), :],
                loc_sem.at[4 + t * KVH + g]))
    loads.append(pltpu.make_async_copy(q_hbm, qraw, loc_sem.at[12]))
    for cp in loads:
        cp.start()
    barrier = pltpu.get_barrier_semaphore()
    def at(dz, d):
        return (((y + d) % NY) * NZ + (z + NZ + dz) % NZ, blk)

    near = [at(dz, d) for dz in COLS for d in range(NY) if dz or d] + xdev[1:] + [mate]
    for dev in near:
        pl.semaphore_signal(barrier, inc=1, device_id=dev, device_id_type=MESH)

    shape = (8, PAGES_REQ)
    lane = lax.broadcasted_iota(jnp.int32, shape, 1)
    row8 = lax.broadcasted_iota(jnp.int32, shape, 0)
    owners_v = jnp.broadcast_to(own_v[...], shape)
    seen = jnp.zeros(shape, jnp.int32)
    rank = jnp.zeros(shape, jnp.int32)
    page0 = jnp.zeros(shape, jnp.int32)
    page1 = jnp.zeros(shape, jnp.int32)
    for s in range(PAGES_REQ):
        o, ident = own_s[0, s], ids_s[0, s]
        hit = lane == o
        page0 = jnp.where(hit & (seen == 0), ident, page0)
        page1 = jnp.where(hit & (seen == 1), ident, page1)
        seen = seen + hit.astype(jnp.int32)
        rank = rank + ((owners_v == o) & (lane > s)).astype(jnp.int32)
    dd = ((owners_v >> 3) - y + NY) & (NY - 1)
    kk = (z - (owners_v & 7) + NZ) & (NZ - 1)
    jj = jnp.where(kk == 0, 0, jnp.where(kk < 4, 2 * kk - 1, jnp.where(kk == 4, 7, 2 * (8 - kk))))
    where_v = (dd * NZ + jj) * 2 + jnp.minimum(rank, 1)
    table = jnp.where(row8 == 0, page0 + PAGES_DEV * page1, where_v)
    ltab[0, 0] = jnp.zeros((1, 128), jnp.int32)
    ltab[0, 0, :, 0:PAGES_REQ] = table[0:1]
    wtab[...] = jnp.zeros((1, 128), jnp.int32)
    wtab[:, 0:PAGES_REQ] = table[1:2]

    limit = len_s[0]
    for cp in loads[:12]:
        cp.wait()
    pl.semaphore_wait(barrier, len(near))

    def prepare():
        rowk = lax.broadcasted_iota(jnp.int32, (KC, DH), 0)
        am[0] = jnp.where(rowk // QB <= blk, 1.0, 0.0).astype(BF)
        for grp in range(2):
            within = rowk % CK
            pos = (within // CR) * PAGE + (grp * 2 + rowk // CK) * CR + within % CR
            am[1 + grp] = jnp.where(pos < limit, 1.0, 0.0).astype(BF)

        @pl.loop(0, KVH)
        def _(g):
            acc[g] = jnp.zeros((ROWS, 2 * DH), F32)
            top[g] = jnp.full((ROWS, DH), -1e30, F32)

        loads[12].wait()
        for hd in range(KVH * 8):
            qs = qraw[:, hd * DH:(hd + 1) * DH].astype(F32) * SCALE
            hi = qs.astype(BF)
            rows = pl.ds((hd % 8) * QB, QB)
            q2[hd // 8, rows, 0:DH] = hi
            q2[hd // 8, rows, DH:2 * DH] = (qs - hi.astype(F32)).astype(BF)
        for j in range(1, 8):
            @pl.when(j > blk)
            def _():
                for g in range(KVH):
                    first = kvall[0, g, 0, 0:1, :]
                    kvall[0, g, 0, pl.ds(j * QB, QB), :] = jnp.broadcast_to(first, (QB, DH))
                    kvall[0, g, 1, pl.ds(j * QB, QB), :] = jnp.zeros((QB, DH), BF)

    def span_part(j):
        return kvall.at[0, :, :, pl.ds(pl.multiple_of(j * QB, QB), QB), :]

    def span_send(i):
        return rcopy(span_part(0), span_part(2 * i), sp_ss.at[i], sp_rs.at[i], xdev[i])

    def span_mate(i):
        return rcopy(span_part(2 * i), span_part(2 * i + 1 - 2 * c), spp_ss.at[i], spp_rs.at[i], mate)

    def span_start():
        for i in (1, 2, 3):
            @pl.when(x + i < NX)
            def _():
                span_send(i).start()

        @pl.when(c == 0)
        def _():
            span_mate(0).start()

    def span_pass(i):
        @pl.when(x >= i)
        def _():
            span_send(i).wait_recv()
            span_mate(i).start()

    def span_done():
        @pl.when(c == 1)
        def _():
            rcopy(span_part(0), span_part(1), spp_ss.at[0], spp_rs.at[0], mate).wait_recv()
        for i in (1, 2, 3):
            @pl.when(x >= i)
            def _():
                rcopy(span_part(2 * i), span_part(2 * i - 1 + 2 * c), spp_ss.at[i], spp_rs.at[i], mate).wait_recv()

    def list_send(col, d):
        ss, rs = (list_ss.at[0], list_rs.at[0]) if col == 0 else (list_ss.at[1], list_rs.at[1])
        return rcopy(ltab.at[0, 0], ltab.at[col, d], ss, rs, at(-COLS[col], d))

    def lists_start():
        for col in range(len(COLS)):
            for d in range(NY):
                if col or d:
                    list_send(col, d).start()

    def lists_wait(recv):
        for i, part in ((0, ltab.at[0, pl.ds(1, NY - 1)]), (1, ltab.at[pl.ds(1, 4)])):
            cp = rcopy(part, part, list_ss.at[i], list_rs.at[i], mate)
            if recv:
                cp.wait_recv()
            else:
                cp.wait_send()

    def tables():
        lists_wait(True)
        cps = [pltpu.make_async_copy(ltab, tab, tab_sem.at[0]), pltpu.make_async_copy(wtab, wtab_s, tab_sem.at[1])]
        for cp in cps:
            cp.start()
        for cp in cps:
            cp.wait()

    def z_up(h, k):
        return rcopy(zb[h][k], zb[h][k + 1], z_ss.at[h], z_rs.at[h, k + 1], zr)

    def z_down(h, k):
        return rcopy(zb[h][(NZ - k) % NZ], zb[h][NZ - k - 1], z_ss.at[h], z_rs.at[h, NZ - k - 1], zl)

    def y_send(h, e, d):
        lo = 0 if e == 0 else 2 * (2 * e - 1)
        part = pl.ds(lo, 2 * len(GROUPS[e]))
        return rcopy(ysend[h].at[d, part], rbuf[h].at[d, part], y_ss.at[h], y_rs.at[h], at(0, NY - d))

    def f_send(h, lo, n, col, d):
        return rcopy(fsend[h].at[d, pl.ds(lo, n)], rbuf[h].at[d, pl.ds(NEAR + lo, n)], f_ss.at[h], f_rs.at[h],
                     at(COLS[col], NY - d))

    def pack(h, e):
        pages = {}
        for k in GROUPS[e]:
            owner = y * NZ + (z + NZ - k) % NZ
            for d in range(NY):
                for slot in range(2):
                    both = tab[0, d, 0, owner]
                    pages[k, d, slot] = both >> 4 if slot else both & 15
        got = {key: zb[h][key[0]][page] for key, page in pages.items()}
        for (k, d, slot), value in got.items():
            dst = rbuf[h].at[0] if d == 0 else ysend[h].at[d]
            dst[2 * PLACE_OF[k] + slot] = value
        for d in range(1, NY):
            y_send(h, e, d).start()

    def pack_far(h):
        pages = {}
        for d in range(NY):
            for i, (k, col, slot) in enumerate(FAR_SLOTS):
                both = tab[col, d, 0, y * NZ + (z + NZ - k) % NZ]
                pages[d, i] = both >> 4 if slot else both & 15
        got = {key: zb[h][FAR_SLOTS[key[1]][0]][page] for key, page in pages.items()}
        for (d, i), value in got.items():
            fsend[h][d, i] = value
        for lo, n, col in FAR_RUNS:
            for d in range(NY):
                f_send(h, lo, n, col, d).start()

    def own(h):
        z_up(h, 0).start()
        z_down(h, 0).start()

    def ring(h, k):
        z_up(h, k - 1).wait_recv()
        if k == 1:
            z_up(h, 1).start()
        z_down(h, k - 1).wait_recv()
        if k == 1:
            z_down(h, 1).start()

    def part(h, r):
        g = (x + NX - r) % NX
        return lambda t, half=None: kvall.at[
            1 + h // 2, g, t,
            pl.ds((h % 2) * CK + (0 if half is None else half * (CK // 2)), CK if half is None else CK // 2), :]

    def x_send(h, up):
        mine = part(h, 0)(c)
        return rcopy(mine, mine, x_ss.at[h], x_rs.at[h, 0 if up else 1], xdev[1] if up else xdev[3])

    def x_recv(h, up):
        got = part(h, 1 if up else 3)(c)
        return rcopy(got, got, x_ss.at[h], x_rs.at[h, 0 if up else 1], xdev[1])

    def x_pass(h, up):
        got = part(h, 1 if up else 3)(c, 0 if up else 1)
        return rcopy(got, got, x_ss.at[h], x_rs.at[h, 2 if up else 3], xdev[1] if up else xdev[3])

    def x_far(h, up):
        got = part(h, 2)(c, 0 if up else 1)
        return rcopy(got, got, x_ss.at[h], x_rs.at[h, 2 if up else 3], xdev[1])

    def m_send(h, r):
        mine = part(h, r)(c)
        return rcopy(mine, mine, p_ss.at[h], p_rs.at[h, r], mate)

    def m_recv(h, r):
        got = part(h, r)(1 - c)
        return rcopy(got, got, p_ss.at[h], p_rs.at[h, r], mate)

    def compact(h):
        part_in = rbuf[h].at[pl.ds(1, NY - 1), pl.ds(0, NEAR)]
        rcopy(part_in, part_in, y_ss.at[h], y_rs.at[h], mate).wait_recv()
        part_in = rbuf[h].at[:, pl.ds(NEAR, FAR)]
        rcopy(part_in, part_in, f_ss.at[h], f_rs.at[h], mate).wait_recv()
        grp, base = 1 + h // 2, (h % 2) * CK
        rows = lax.broadcasted_iota(jnp.int32, (CR, DH), 0)
        fill = None
        places = [wtab_s[0, s] for s in range(PAGES_REQ)]
        pages = [rbuf[h][place >> 4, place & 15] for place in places]
        for s, page in enumerate(pages):
            if s == 0:
                fill = jnp.broadcast_to(page[0:1].astype(F32), (CR, DH)) * (1 - c).astype(F32)
            if s >= SURE:
                page = jnp.where(rows < limit - (s * PAGE + h * CR), page.astype(F32), fill).astype(BF)
            kvall[grp, x, c, pl.ds(base + s * CR, CR), :] = page
        x_send(h, True).start()
        x_send(h, False).start()
        m_send(h, 0).start()

    def neighbours(h):
        x_recv(h, True).wait_recv()
        x_pass(h, True).start()
        x_recv(h, False).wait_recv()
        x_pass(h, False).start()
        m_send(h, 1).start()
        m_send(h, 3).start()

    def opposite(h):
        x_far(h, True).wait_recv()
        x_far(h, False).wait_recv()
        m_send(h, 2).start()

    def R(h, k): return lambda: ring(h, k)
    def Q(h, e): return lambda: pack(h, e)
    def Z(h): return lambda: pack_far(h)
    def O(h): return lambda: own(h)
    def C(h): return lambda: compact(h)
    def N(h): return lambda: neighbours(h)
    def F(h): return lambda: opposite(h)
    def SP(i): return lambda: span_pass(i)

    plan = PLAN(R, Q, Z, O, C, N, F, SP, span_done, lists_start, span_start, tables, prepare)
    for step in plan[-1]:
        step()

    @pl.loop(0, 12)
    def _(u):
        grp = u // 4
        i = u % 4
        r = i + i // 2 - 2 * (i // 3)
        g = (x + NX - r) % NX

        def hook(place):
            for at, steps in plan.items():
                if at >= 0 and at % 4 == place:
                    @pl.when(u == at // 4)
                    def _():
                        for step in steps:
                            step()

        hook(0)
        for uu in range(4, 12):
            @pl.when(u == uu)
            def _():
                rr = (0, 1, 3, 2)[uu % 4]
                for h in (0, 1):
                    m_recv((uu // 4 - 1) * 2 + h, rr).wait_recv()
        keys = kvall[grp, g, 0]
        vals = kvall[grp, g, 1]
        k2 = jnp.concatenate([keys, keys], axis=1)
        v2 = jnp.concatenate([vals, am[grp]], axis=1)
        token = lax.broadcasted_iota(jnp.int32, (RB, QB), 0) % QB
        key = lax.broadcasted_iota(jnp.int32, (RB, QB), 1)
        inside = (key <= token) | (grp > 0)

        def scores(rb):
            s = dot(q2[g, pl.ds(rb * RB, RB), :], k2, 1, 1)
            return jnp.concatenate([jnp.where(inside, s[:, :QB], -1e30), s[:, QB:]], axis=1)

        def granule(rb, s):
            rows = pl.ds(rb * RB, RB)
            old = top[g, rows, 0:1]
            new = jnp.maximum(old, jnp.max(s, axis=1, keepdims=True))
            p = jnp.exp2(s - new).astype(BF)
            acc[g, rows, :] = acc[g, rows, :] * jnp.exp2(old - new) + dot(p, v2, 1, 0)
            top[g, rows, :] = jnp.broadcast_to(new, (RB, DH))

        n = ROWS // RB
        for pair in range(n // 2):
            if pair:
                hook(pair * 2)
            s0 = scores(2 * pair)
            s1 = scores(2 * pair + 1)
            granule(2 * pair, s0)
            granule(2 * pair + 1, s1)

        @pl.when(grp == 2)
        def _():
            for hd in range(8):
                a = acc[g, pl.ds(hd * QB, QB), :]
                out_ref[:, pl.ds(pl.multiple_of((g * 8 + hd) * DH, DH), DH)] = (
                    a[:, :DH] / a[:, DH:]).astype(BF)

    lists_wait(False)
    for i in (1, 2, 3):
        @pl.when(x + i < NX)
        def _():
            span_send(i).wait_send()

        @pl.when(x >= i)
        def _():
            span_mate(i).wait_send()

    @pl.when(c == 0)
    def _():
        span_mate(0).wait_send()
    for h in range(CH):
        for ref, ss in (
            (kvall.at[1, pl.ds(0, 3), 0, pl.ds(0, CK), :], x_ss.at[h]),
            (kvall.at[1, :, 0, pl.ds(0, CK), :], p_ss.at[h]),
            (ysend[h].at[pl.ds(1, NY - 1)], y_ss.at[h]),
            (fsend[h], f_ss.at[h]),
        ):
            rcopy(ref, ref, ss, ss, mate).wait_send()
        z_wait = kvall.at[1, 0, 0, pl.ds(0, 4 * PAGES_DEV * CR), :]
        rcopy(z_wait, z_wait, z_ss.at[h], z_ss.at[h], mate).wait_send()


def PLAN(R, Q, Z, O, C, N, F, SP, SD, LS, SS, LT, PR):
    return {
        -1: [O(0), LS, SS, O(1), PR, R(0, 1), LT, O(2), Q(0, 0), Q(0, 1), R(1, 1), O(3), R(0, 2), Q(0, 2), Z(0), Q(1, 0), Q(1, 1), R(2, 1), Q(2, 0), Q(2, 1), R(1, 2), Q(1, 2), Z(1), R(3, 1), Q(3, 0), Q(3, 1), SP(1), SP(3), SP(2), C(0), R(2, 2), Q(2, 2), Z(2), SD],
        0: [R(3, 2), Q(3, 2), Z(3)],
        4: [C(1)],
        8: [N(0)],
        12: [C(2)],
        16: [N(1), F(0)],
        18: [C(3)],
        24: [N(2), F(1)],
        28: [N(3)],
        30: [F(2)],
        34: [F(3)],
    }


def per_device(queries, span_kv, kv_store, page_ids, page_owner, prefix_len):
    anyw = pl.BlockSpec(memory_space=pl.ANY)
    smem = pl.BlockSpec(memory_space=pltpu.SMEM)
    vmem = pl.BlockSpec(memory_space=pltpu.VMEM)
    dma = pltpu.SemaphoreType.DMA
    scratch = [pltpu.VMEM((PAGES_DEV, CR, DH), BF) for _ in range(CH * 5)]
    scratch += [pltpu.VMEM((NY, NEAR, CR, DH), BF) for _ in range(CH)]
    scratch += [pltpu.VMEM((NY, FAR, CR, DH), BF) for _ in range(CH)]
    scratch += [pltpu.VMEM((NY, NEAR + FAR, CR, DH), BF) for _ in range(CH)]
    scratch += [
        pltpu.VMEM((3, KVH, 2, KC, DH), BF),
        pltpu.VMEM((3, KC, DH), BF),
        pltpu.VMEM((QB, KVH * 8 * DH), BF),
        pltpu.VMEM((KVH, ROWS, 2 * DH), BF),
        pltpu.VMEM((KVH, ROWS, 2 * DH), F32),
        pltpu.VMEM((KVH, ROWS, DH), F32),
        pltpu.VMEM((len(COLS), NY, 1, 128), jnp.int32),
        pltpu.SMEM((len(COLS), NY, 1, 128), jnp.int32),
        pltpu.VMEM((1, 128), jnp.int32),
        pltpu.SMEM((1, 128), jnp.int32),
        dma((13,)), dma((2,)), dma((2,)), dma((2,)),
        dma((CH,)), dma((CH, NZ)),
        dma((CH,)), dma((CH,)), dma((CH,)), dma((CH,)),
        dma((CH,)), dma((CH, 4)),
        dma((CH,)), dma((CH, 4)),
        dma((4,)), dma((4,)), dma((4,)), dma((4,)),
    ]
    return pl.pallas_call(
        kernel,
        out_shape=jax.ShapeDtypeStruct(queries.shape, BF),
        in_specs=[smem, smem, smem, vmem, anyw, anyw, anyw],
        out_specs=vmem,
        scratch_shapes=scratch,
        compiler_params=pltpu.CompilerParams(
            vmem_limit_bytes=56 * 2**20, collective_id=0, has_side_effects=True),
        cost_estimate=pl.CostEstimate(
            flops=4 * 4096 * 3072 * 128, bytes_accessed=4 * 2**20, transcendentals=4096 * 3072),
    )(page_owner, page_ids, prefix_len, page_owner, queries, span_kv, kv_store)


def solution(mesh):
    in_specs = (
        P(("pool", "blk"), None),
        P(("pool", "blk"), None),
        P("pool", None, None),
        P("pool", None),
        P("pool", None),
        P("pool"),
    )
    return jax.shard_map(
        per_device, mesh=mesh, in_specs=in_specs, out_specs=P(("pool", "blk"), None), check_vma=False
    )
```
